32 devices in a mesh: pair: 4 (over y, x), grid: 8 (over z, core).
Axes of the slice: x: 2, y: 2, z: 4, core: 2. Of those that a mesh axis runs over, the one named last changes fastest.
Arguments:
- cycle_matrix: bfloat16 [24576, 24576], P('grid', 'pair'), may hold values from -0.0390625 to 0.0390625
- amplitudes: bfloat16 [256, 24576], P(None, ('pair', 'grid')), may hold values from -6 to 6
- fit_panel: bfloat16 [4, 384, 1024], P(None, 'grid', 'pair'), may hold values from -0.1875 to 0.1875
- pair_amps: bfloat16 [1024, 384, 384], P('pair', 'grid'), may hold values from -0.59765625 to 0.59765625
- pair_list: int32 [1024], P('pair'), may hold values from 0 to 4095, as said below
- window_list: int32 [384], replicated, may hold values from 0 to 383, each once
- occ_energy: float32 [64], replicated, may hold values from -2 to -0.5
- vir_energy: float32 [384], replicated, may hold values from 0.5 to 3
Outputs:
- cycle_update: bfloat16 [256, 24576], P('pair', 'grid')
- ladder_update: float32 [1024, 16], P('pair')
The draws below stay inside these ranges and needn't reach their ends.
Inputs may be any that keep to these rules, and one draw needn't show every extreme that they name: `pair_list`: distinct pair indices i * 64 + j. `window_list`: each virtual orbital once.
All inputs are finite; a program needn't handle non-finite values.
Results may differ from the reference program's by a relative error of at most 0.0031.
Values may be sent and summed in bfloat16 or wider, within the bound.
A program may use at most 128 MiB of HBM per device.

```python
import jax
import jax.numpy as jnp

O = 64
V = 384
NAUX = 1024
W = 4
PAIRS = 1024
COLS = 256


def draw_pair_list(key, part):
    return jax.random.permutation(key, O * O)[:PAIRS].astype(jnp.int32)


def block_levels(key, shape, pieces, least, top_value):
    level, own = 1.0, jax.random.fold_in(key, 6)
    for dim, parts in pieces:
        steps = jnp.exp(jax.random.uniform(jax.random.fold_in(own, dim), (parts,), jnp.float32, least / len(pieces), top_value / len(pieces)))
        level = level * jnp.repeat(steps, shape[dim] // parts).reshape([-1 if axis == dim else 1 for axis in range(len(shape))])
    return level


def gaussian(key, dims, width, limit, shards=(), kind=jnp.bfloat16):
    values = jax.random.normal(key, dims, jnp.float32) * width
    if len(shards) > 0:
        values = block_levels(key, dims, shards, -0.22, 0.18) * values
    return jnp.clip(values, min=-limit, max=limit).astype(kind)


def setup_inputs(seed: int = 0) -> dict:
    streams_of = jax.random.split(jax.random.key(seed), 9)
    return {
        "cycle_matrix": gaussian(streams_of[0], (O * V, O * V), (O * V) ** -0.5, 0.0390625, ((0, 8), (1, 4))),
        "amplitudes": gaussian(streams_of[1], (COLS, O * V), 1.0, 6.0, ((1, 32),)),
        "fit_panel": gaussian(streams_of[2], (W, V, NAUX), NAUX ** -0.5, 0.1875, ((1, 8), (2, 4))),
        "pair_amps": gaussian(streams_of[3], (PAIRS, V, V), 0.1, 0.59765625, ((0, 4), (1, 8))),
        "pair_list": draw_pair_list(jax.random.fold_in(streams_of[8], 71), 0),
        "window_list": jax.random.permutation(streams_of[5], V).astype(jnp.int32),
        "occ_energy": jnp.clip(jax.random.uniform(streams_of[6], (O,), jnp.float32, -2.0, -0.5), -2.0, -0.5),
        "vir_energy": jnp.clip(jax.random.uniform(streams_of[7], (V,), jnp.float32, 0.5, 3.0), 0.5, 3.0),
    }


def reference(cycle_matrix, amplitudes, fit_panel, pair_amps, pair_list, window_list, occ_energy, vir_energy):
    ewin = vir_energy[window_list[:W]]
    cycle = jnp.dot(amplitudes, cycle_matrix.T, preferred_element_type=jnp.float32)
    column_ids = jnp.arange(O * W, dtype=jnp.int32)
    row_ids = jnp.arange(O * V, dtype=jnp.int32)
    col_energy = occ_energy[column_ids // W] - ewin[column_ids % W]
    row_energy = occ_energy[row_ids // V] - vir_energy[row_ids % V]
    cycle_update = (cycle / (col_energy[:, None] + row_energy[None, :])).astype(jnp.bfloat16)
    panel = fit_panel.astype(jnp.float32)
    tile = jnp.einsum('acq,bdq->abcd', panel, panel).astype(jnp.bfloat16)
    ladder = jnp.dot(pair_amps.reshape(pair_amps.shape[0], V * V), tile.reshape(W * W, V * V).T, preferred_element_type=jnp.float32)
    pair_energy = occ_energy[pair_list // O] + occ_energy[pair_list % O]
    win_pair = (ewin[:, None] + ewin[None, :]).reshape(W * W)
    ladder_update = ladder / (pair_energy[:, None] - win_pair[None, :])
    return cycle_update, ladder_update
```

```python
import functools

import jax
import jax.numpy as jnp
from jax import lax
from jax.experimental import pallas as pl
from jax.experimental.pallas import tpu as pltpu
from jax.sharding import PartitionSpec as P

O = 64
V = 384
W = 4
CHUNKS = 4
SUB = 16
MESH = pl.DeviceIdType.MESH
NT = (((1,), (1,)), ((), ()))


def lookup(table, index):
    hits = index[:, None] == jnp.arange(table.shape[0], dtype=jnp.int32)[None, :]
    return jnp.sum(jnp.where(hits, table[None, :], jnp.float32(0.0)), axis=1)


def dot_nt(a, b):
    return lax.dot_general(a, b, NT, preferred_element_type=jnp.float32)


def kernel(
    n_p, n_g, amps, mat, fit, pairs, cyc_out, lad_out,
    abuf, mbuf, tbuf, xbuf, ybuf, zbuf, wt, sbuf, lbuf, acc, rsend, rrecv,
    msem, lsem, arecv, asend, xrecv, xsend, zrecv, zsend, rrsem, rssem, lrecv, lsend,
):
    n_z = n_g // 2
    p = lax.axis_index("pair")
    g = lax.axis_index("grid")
    z = g // 2
    c = g % 2
    sib = z * 2 + 1 - c
    rows = abuf.shape[2]
    depth = abuf.shape[3]
    h = rows // CHUNKS
    cols = mbuf.shape[1]
    own_c = ybuf.shape[2]
    n_pairs = tbuf.shape[0]
    item_y = CHUNKS
    tile_n = 512 if cols % 512 == 0 else cols
    q_of = [lax.rem(p + k, n_p) for k in range(1, n_p)]
    g_of = [lax.rem(g + k, n_g) for k in range(1, n_g)]

    load_x = pltpu.make_async_copy(fit, xbuf.at[p], lsem.at[0])
    load_x.start()
    load_a = pltpu.make_async_copy(amps, abuf.at[g], lsem.at[1])
    load_a.start()

    def load_m(s):
        at = pl.multiple_of(s * depth, 128)
        return pltpu.make_async_copy(mat.at[:, pl.ds(at, depth)], mbuf.at[s], msem.at[s])

    load_m(g).start()
    load_m(sib).start()
    for t in range(1, n_z):
        for d in (1, -1):
            sz = z - d * t

            @pl.when(jnp.logical_and(sz >= 0, sz < n_z))
            def _():
                load_m(sz * 2 + c).start()
                load_m(sz * 2 + 1 - c).start()
    load_t = pltpu.make_async_copy(pairs, tbuf, lsem.at[2])
    load_t.start()

    barrier = pltpu.get_barrier_semaphore()
    for q in q_of:
        pl.semaphore_signal(barrier, inc=1, device_id={"pair": q}, device_id_type=MESH)
    for q in g_of:
        pl.semaphore_signal(barrier, inc=1, device_id={"grid": q}, device_id_type=MESH)
    pl.semaphore_wait(barrier, n_p - 1 + n_g - 1)

    def shard(item, s):
        if item == item_y:
            return ybuf.at[:, s]
        return abuf.at[s, :, pl.ds(item * h, h), :]

    def hop(item, s, kind, target):
        ref = shard(item, s)
        return pltpu.make_async_remote_copy(
            src_ref=ref, dst_ref=ref, send_sem=asend.at[item, s, kind], recv_sem=arecv.at[item, s],
            device_id={"grid": target}, device_id_type=MESH,
        )

    def own_send(item, act):
        @pl.when(z + 1 < n_z)
        def _():
            act(hop(item, g, 0, g + 2))

        @pl.when(z >= 1)
        def _():
            act(hop(item, g, 2, g - 2))

        act(hop(item, g, 1, sib))

    def each_line(t, body):
        for d in (1, -1):
            sz = z - d * t

            @pl.when(jnp.logical_and(sz >= 0, sz < n_z))
            def _():
                body(d, sz)

    def forward(item, t, wait_first, act):
        def body(d, sz):
            s = sz * 2 + c
            if wait_first:
                hop(item, s, 0, sib).wait_recv()
            nz = z + d

            @pl.when(jnp.logical_and(nz >= 0, nz < n_z))
            def _():
                act(hop(item, s, 0, nz * 2 + c))

            act(hop(item, s, 1, sib))

        each_line(t, body)

    def begin(cp):
        cp.start()

    def product(r, s, first=False):
        if r == 0:
            load_m(s).wait()

        def tile(i, carry):
            at = pl.ds(pl.multiple_of(i * tile_n, 128), tile_n)
            lhs = abuf[s, :, r * h:(r + 1) * h, :].reshape(n_p * h, depth)
            out = dot_nt(lhs, mbuf[s, at, :]).reshape(n_p, h, tile_n)
            if first:
                acc[r, :, :, at] = out
            else:
                acc[r, :, :, at] += out
            return carry

        lax.fori_loop(0, cols // tile_n, tile, 0)

    def scatter(r, k):
        q = q_of[k]
        return pltpu.make_async_remote_copy(
            src_ref=rsend.at[r, q], dst_ref=rrecv.at[p, r], send_sem=rssem.at[r, k],
            recv_sem=rrsem.at[r, p], device_id={"pair": q}, device_id_type=MESH,
        )

    def scatter_wait(r, q):
        pltpu.make_async_remote_copy(
            src_ref=rsend.at[r, q], dst_ref=rrecv.at[q, r], send_sem=rssem.at[r, 0],
            recv_sem=rrsem.at[r, q], device_id={"pair": q}, device_id_type=MESH,
        ).wait_recv()

    def reduce_start(r):
        rsend[r] = acc[r].astype(rsend.dtype)
        for k in range(n_p - 1):
            scatter(r, k).start()

    def reduce_end(r):
        total = acc[r, p]
        for q in q_of:
            scatter_wait(r, q)
            total = total + rrecv[q, r].astype(jnp.float32)
        cyc_out[r * h:(r + 1) * h, :] = total

    def spread(buf, slot, send, recv, k):
        q = q_of[k]
        return pltpu.make_async_remote_copy(
            src_ref=buf.at[slot], dst_ref=buf.at[slot], send_sem=send.at[k], recv_sem=recv.at[slot],
            device_id={"pair": q}, device_id_type=MESH,
        )

    def spread_all(buf, send, recv):
        for k in range(n_p - 1):
            spread(buf, p, send, recv, k).start()

    def spread_wait(buf, send, recv):
        for k in range(n_p - 1):
            spread(buf, q_of[k], send, recv, k).wait_recv()

    def tile_part():
        total = None
        for q in range(n_p):
            term = dot_nt(xbuf[q], ybuf[q].reshape(n_g * own_c, ybuf.shape[3]))
            total = term if total is None else total + term
        zbuf[p] = total.astype(zbuf.dtype)

    def weights():
        for j in range(own_c // SUB):
            for a in range(W):
                for b in range(W):
                    at = (a * W + b) * SUB
                    wt[j, at:at + SUB, :] = zbuf[b, a * own_c + j * SUB:a * own_c + (j + 1) * SUB, :]

    piece = n_pairs // n_z

    def ladder_piece(i):
        at = pl.ds(pl.multiple_of(i * piece, 8), piece)
        total = None
        for j in range(own_c // SUB):
            lhs = tbuf[at, j * SUB:(j + 1) * SUB, :].reshape(piece * SUB, tbuf.shape[2])
            term = dot_nt(lhs, wt[j])
            total = term if total is None else total + term
        total = total.reshape(piece, SUB, W * W * SUB)
        r_id = lax.broadcasted_iota(jnp.int32, (1, SUB, W * W * SUB), 1)
        c_id = lax.broadcasted_iota(jnp.int32, (1, SUB, W * W * SUB), 2)
        sbuf[at, :] = jnp.sum(jnp.where(r_id == c_id % SUB, total, 0.0), axis=1)

    def lad_copy(k, slot):
        return pltpu.make_async_remote_copy(
            src_ref=lbuf.at[slot], dst_ref=lbuf.at[slot], send_sem=lsend.at[k], recv_sem=lrecv.at[slot],
            device_id={"grid": g_of[k]}, device_id_type=MESH,
        )

    def ladder_send():
        row = lax.broadcasted_iota(jnp.int32, (W * W, W * W * SUB), 0)
        col = lax.broadcasted_iota(jnp.int32, (W * W, W * W * SUB), 1)
        ones = jnp.where(row == col // SUB, 1.0, 0.0).astype(jnp.float32)
        lbuf[g] = lax.dot_general(
            ones, sbuf[...], NT, precision=lax.Precision.HIGHEST, preferred_element_type=jnp.float32
        )
        for k in range(n_g - 1):
            lad_copy(k, g).start()

    def ladder_end():
        for k in range(n_g - 1):
            lad_copy(k, g_of[k]).wait_recv()
        total = lbuf[0]
        for s in range(1, n_g):
            total = total + lbuf[s]
        lad_out[...] = total

    def chunk(r, extra):
        if r + 1 < CHUNKS:
            own_send(r + 1, begin)
        product(r, g, first=True)
        if r == 0:
            spread_wait(xbuf, xsend, xrecv)
            mine = pl.ds(pl.multiple_of(p * own_c, SUB), own_c)
            ybuf[:, g] = xbuf[:, mine, :]
            own_send(item_y, begin)
        hop(r, sib, 1, sib).wait_recv()
        product(r, sib)

        def step(t, carry):
            forward(r, t, True, begin)
            if r == 0:
                forward(item_y, t, True, begin)
            if extra is not None:
                extra(t)

            def use(d, sz):
                product(r, sz * 2 + c)
                s = sz * 2 + 1 - c
                hop(r, s, 1, sib).wait_recv()
                product(r, s)

            each_line(t, use)
            return carry

        lax.fori_loop(1, n_z, step, 0)
        reduce_start(r)

    load_x.wait()
    spread_all(xbuf, xsend, xrecv)
    load_a.wait()
    own_send(0, begin)
    chunk(0, None)
    hop(item_y, sib, 1, sib).wait_recv()

    def rest(t, carry):
        each_line(t, lambda d, sz: hop(item_y, sz * 2 + 1 - c, 1, sib).wait_recv())
        return carry

    lax.fori_loop(1, n_z, rest, 0)
    tile_part()
    spread_all(zbuf, zsend, zrecv)
    chunk(1, None)
    reduce_end(0)
    spread_wait(zbuf, zsend, zrecv)
    weights()
    load_t.wait()
    for r in range(2, CHUNKS):
        if r == 2:
            chunk(r, ladder_piece)
            ladder_piece(0)
            ladder_send()
        else:
            chunk(r, None)
        if r + 1 < CHUNKS:
            reduce_end(r - 1)
    ladder_end()
    reduce_end(CHUNKS - 2)
    reduce_end(CHUNKS - 1)

    def sent(cp):
        cp.wait_send()

    for item in range(CHUNKS + 1):
        own_send(item, sent)

        def step(t, carry, item=item):
            forward(item, t, False, sent)
            return carry

        lax.fori_loop(1, n_z, step, 0)
    for k in range(n_p - 1):
        spread(xbuf, p, xsend, xrecv, k).wait_send()
        spread(zbuf, p, zsend, zrecv, k).wait_send()
        for r in range(CHUNKS):
            scatter(r, k).wait_send()
    for k in range(n_g - 1):
        lad_copy(k, g).wait_send()


def fused(n_p, n_g, amplitudes, cycle_matrix, fit_panel, pair_amps):
    rows = amplitudes.shape[0] // n_p
    depth = amplitudes.shape[1]
    cols = cycle_matrix.shape[0]
    n_pairs, own_c, n_v = pair_amps.shape
    aux = fit_panel.shape[2]
    h = rows // CHUNKS
    bf, f32 = jnp.bfloat16, jnp.float32
    dma = pltpu.SemaphoreType.DMA
    hbm = pl.BlockSpec(memory_space=pl.ANY)
    vmem = pl.BlockSpec(memory_space=pltpu.VMEM)
    return pl.pallas_call(
        functools.partial(kernel, n_p, n_g),
        out_shape=(
            jax.ShapeDtypeStruct((rows, cols), f32),
            jax.ShapeDtypeStruct((W * W, n_pairs), f32),
        ),
        in_specs=[hbm] * 4,
        out_specs=(vmem, vmem),
        scratch_shapes=[
            pltpu.VMEM((n_g, n_p, rows, depth), bf),
            pltpu.VMEM((n_g, cols, depth), bf),
            pltpu.VMEM((n_pairs, own_c, n_v), bf),
            pltpu.VMEM((n_p, W * own_c, aux), bf),
            pltpu.VMEM((n_p, n_g, own_c, aux), bf),
            pltpu.VMEM((n_p, W * own_c, n_v), bf),
            pltpu.VMEM((own_c // SUB, W * W * SUB, n_v), bf),
            pltpu.VMEM((n_pairs, W * W * SUB), f32),
            pltpu.VMEM((n_g, W * W, n_pairs), f32),
            pltpu.VMEM((CHUNKS, n_p, h, cols), f32),
            pltpu.VMEM((CHUNKS, n_p, h, cols), bf),
            pltpu.VMEM((n_p, CHUNKS, h, cols), bf),
            dma((n_g,)),
            dma((3,)),
            dma((CHUNKS + 1, n_g)),
            dma((CHUNKS + 1, n_g, 3)),
            dma((n_p,)),
            dma((n_p,)),
            dma((n_p,)),
            dma((n_p,)),
            dma((CHUNKS, n_p)),
            dma((CHUNKS, n_p)),
            dma((n_g,)),
            dma((n_g,)),
        ],
        compiler_params=pltpu.CompilerParams(
            collective_id=0, has_side_effects=True, vmem_limit_bytes=63 * 1024 * 1024
        ),
    )(
        amplitudes.reshape(n_p, rows, depth),
        cycle_matrix,
        fit_panel.reshape(W * own_c, aux),
        pair_amps,
    )


def plain(n_p, n_g, amplitudes, cycle_matrix, fit_panel, pair_amps):
    partial_cycle = lax.dot_general(
        lax.all_gather(amplitudes, "grid", axis=1, tiled=True),
        cycle_matrix,
        NT,
        preferred_element_type=jnp.float32,
    )
    cycle_sum = lax.psum_scatter(partial_cycle, "pair", scatter_dimension=0, tiled=True)
    full_aux = lax.all_gather(fit_panel, "pair", axis=2, tiled=True)
    tile = jnp.einsum(
        "acq,bdq->abcd",
        full_aux,
        lax.all_gather(full_aux, "grid", axis=1, tiled=True),
        preferred_element_type=jnp.float32,
    ).astype(jnp.bfloat16)
    flat_amps = pair_amps.reshape(pair_amps.shape[0], pair_amps.shape[1] * pair_amps.shape[2])
    flat_tile = tile.reshape(W * W, tile.shape[2] * tile.shape[3])
    partial_ladder = lax.dot_general(
        flat_amps, flat_tile, NT, preferred_element_type=jnp.float32
    )
    return cycle_sum, lax.psum(partial_ladder, "grid").T


def suits(n_p, n_g, amplitudes, fit_panel, pair_amps):
    rows = amplitudes.shape[0] // n_p
    return (
        n_p == W
        and n_g % 2 == 0
        and rows % (CHUNKS * SUB) == 0
        and amplitudes.shape[1] % 128 == 0
        and fit_panel.shape[2] % 128 == 0
        and pair_amps.shape[1] % SUB == 0
        and pair_amps.shape[2] % 128 == 0
        and pair_amps.shape[0] % (8 * (n_g // 2)) == 0
    )


def local(
    n_p, n_g,
    cycle_matrix, amplitudes, fit_panel, pair_amps, pair_list, window_list, occ_energy, vir_energy
):
    window_energy = lookup(vir_energy, window_list[:W])
    local_rows = cycle_matrix.shape[0]
    form = fused if suits(n_p, n_g, amplitudes, fit_panel, pair_amps) else plain
    cycle_sum, ladder = form(n_p, n_g, amplitudes, cycle_matrix, fit_panel, pair_amps)
    column_ids = lax.axis_index("pair") * cycle_sum.shape[0] + jnp.arange(
        cycle_sum.shape[0], dtype=jnp.int32
    )
    row_ids = lax.axis_index("grid") * local_rows + jnp.arange(local_rows, dtype=jnp.int32)
    col_energy = lookup(occ_energy, column_ids // W) - lookup(window_energy, column_ids % W)
    row_energy = lookup(occ_energy, row_ids // V) - lookup(vir_energy, row_ids % V)
    cycle_update = (cycle_sum / (col_energy[:, None] + row_energy[None, :])).astype(jnp.bfloat16)
    pair_energy = lookup(occ_energy, pair_list // O) + lookup(occ_energy, pair_list % O)
    win_pair = (window_energy[:, None] + window_energy[None, :]).reshape(W * W)
    ladder_update = ladder.T / (pair_energy[:, None] - win_pair[None, :])
    return (cycle_update, ladder_update)


def solution(mesh):
    return jax.shard_map(
        functools.partial(local, mesh.shape["pair"], mesh.shape["grid"]),
        mesh=mesh,
        in_specs=(
            P("grid", "pair"),
            P(None, ("pair", "grid")),
            P(None, "grid", "pair"),
            P("pair", "grid", None),
            P("pair"),
            P(),
            P(),
            P(),
        ),
        out_specs=(P("pair", "grid"), P("pair", None)),
        check_vma=False,
    )
```

```python
import functools

import jax
import jax.numpy as jnp
from jax import lax
from jax.experimental import pallas as pl
from jax.experimental.pallas import tpu as pltpu
from jax.sharding import PartitionSpec as P

O = 64
V = 384
W = 4
CHUNKS = 2
SUB = 16
MESH = pl.DeviceIdType.MESH
NT = (((1,), (1,)), ((), ()))


def lookup(table, index):
    hits = index[:, None] == jnp.arange(table.shape[0], dtype=jnp.int32)[None, :]
    return jnp.sum(jnp.where(hits, table[None, :], jnp.float32(0.0)), axis=1)


def dot_nt(a, b):
    return lax.dot_general(a, b, NT, preferred_element_type=jnp.float32)


def kernel(
    n_p, n_g, amps, mat, fit, pairs, plist, wlist, occ, vir, cyc_out, lad_out,
    abuf, mbuf, tbuf, xbuf, ybuf, zbuf, wt, sbuf, lbuf, acc, part, rsend, rrecv, cden, rden, lden,
    msem, lsem, arecv, asend, xrecv, xsend, zrecv, zsend, rrsem, rssem, lrecv, lsend,
):
    n_z = n_g // 2
    p = lax.axis_index("pair")
    g = lax.axis_index("grid")
    z = g // 2
    c = g % 2
    sib = z * 2 + 1 - c
    rows = abuf.shape[2]
    depth = abuf.shape[3]
    h = rows // CHUNKS
    cols = mbuf.shape[1]
    own_c = ybuf.shape[2]
    n_pairs = tbuf.shape[0]
    item_y = CHUNKS
    tile_n = tile_of(cols)
    tiles = cols // tile_n
    q_of = [lax.rem(p + k, n_p) for k in range(1, n_p)]
    g_of = [lax.rem(g + k, n_g) for k in range(1, n_g)]

    load_x = pltpu.make_async_copy(fit, xbuf.at[p], lsem.at[0])
    load_x.start()
    load_a = pltpu.make_async_copy(amps, abuf.at[g], lsem.at[1])
    load_a.start()

    def load_m(s):
        at = pl.multiple_of(s * depth, 128)
        return pltpu.make_async_copy(mat.at[:, pl.ds(at, depth)], mbuf.at[s], msem.at[s])

    load_m(g).start()
    load_m(sib).start()
    for t in range(1, n_z):
        for d in (1, -1):
            sz = z - d * t

            @pl.when(jnp.logical_and(sz >= 0, sz < n_z))
            def _():
                load_m(sz * 2 + c).start()
                load_m(sz * 2 + 1 - c).start()
    load_t = pltpu.make_async_copy(pairs, tbuf, lsem.at[2])
    load_t.start()

    barrier = pltpu.get_barrier_semaphore()
    for q in q_of:
        pl.semaphore_signal(barrier, inc=1, device_id={"pair": q}, device_id_type=MESH)
    for q in g_of:
        pl.semaphore_signal(barrier, inc=1, device_id={"grid": q}, device_id_type=MESH)
    pl.semaphore_wait(barrier, n_p - 1 + n_g - 1)

    def shard(item, s):
        if item == item_y:
            return ybuf.at[:, s]
        return abuf.at[s, :, pl.ds(item * h, h), :]

    def hop(item, s, kind, target):
        ref = shard(item, s)
        return pltpu.make_async_remote_copy(
            src_ref=ref, dst_ref=ref, send_sem=asend.at[item, s, kind], recv_sem=arecv.at[item, s],
            device_id={"grid": target}, device_id_type=MESH,
        )

    def own_send(item, act):
        @pl.when(z + 1 < n_z)
        def _():
            act(hop(item, g, 0, g + 2))

        @pl.when(z >= 1)
        def _():
            act(hop(item, g, 2, g - 2))

        act(hop(item, g, 1, sib))

    def each_line(t, body):
        for d in (1, -1):
            sz = z - d * t

            @pl.when(jnp.logical_and(sz >= 0, sz < n_z))
            def _():
                body(d, sz)

    def forward(item, t, wait_first, act):
        def body(d, sz):
            s = sz * 2 + c
            if wait_first:
                hop(item, s, 0, sib).wait_recv()
            nz = z + d

            @pl.when(jnp.logical_and(nz >= 0, nz < n_z))
            def _():
                act(hop(item, s, 0, nz * 2 + c))

            act(hop(item, s, 1, sib))

        each_line(t, body)

    def begin(cp):
        cp.start()

    def product(r, s, first=False):
        if r == 0:
            load_m(s).wait()

        def tile(i, carry):
            at = pl.ds(pl.multiple_of(i * tile_n, 128), tile_n)
            rhs = abuf[s, :, r * h:(r + 1) * h, :].reshape(n_p * h, depth)
            out = dot_nt(mbuf[s, at, :], rhs)
            if first:
                acc[at, :] = out
            else:
                acc[at, :] += out
            return carry

        lax.fori_loop(0, tiles, tile, 0)

    def scatter(r, i, k, q, slot):
        at = slice(i * tile_n, (i + 1) * tile_n)
        return pltpu.make_async_remote_copy(
            src_ref=rsend.at[r, q, :, at], dst_ref=rrecv.at[slot, r, :, at],
            send_sem=rssem.at[r, i, k], recv_sem=rrsem.at[r, i, slot],
            device_id={"pair": q}, device_id_type=MESH,
        )

    def reduce_start(r):
        for i in range(tiles):
            at = slice(i * tile_n, (i + 1) * tile_n)
            block = acc[at, :].T.reshape(n_p, h, tile_n)
            part[r, :, :, at] = block
            rsend[r, :, :, at] = block.astype(rsend.dtype)
            for k in range(n_p - 1):
                scatter(r, i, k, q_of[k], p).start()

    def reduce_end(r):
        for i in range(tiles):
            at = slice(i * tile_n, (i + 1) * tile_n)
            total = part[r, p, :, at]
            for q in q_of:
                scatter(r, i, 0, q, q).wait_recv()
                total = total + rrecv[q, r, :, at].astype(jnp.float32)
            low = cden[r * h:(r + 1) * h, :] + rden[:, at]
            cyc_out[r * h:(r + 1) * h, at] = (total / low).astype(cyc_out.dtype)

    def iota(shape, dim):
        return lax.broadcasted_iota(jnp.int32, shape, dim)

    def pick(hits, values, axis):
        return jnp.sum(jnp.where(hits, values, jnp.zeros_like(values)), axis=axis, keepdims=True)

    def denominators():
        n_o, n_v = occ.shape[1], vir.shape[1]
        occ_row, vir_row = occ[...], vir[...]
        want = pick(iota((W, n_v), 0) == iota((W, n_v), 1), wlist[...], 1)
        ewin_col = pick(iota((W, n_v), 1) == want, vir_row, 1)
        ewin_row = pick(iota((W, W), 0) == iota((W, W), 1), ewin_col, 0)
        occ_col = pick(iota((n_o, n_o), 0) == iota((n_o, n_o), 1), occ_row, 1)
        line = p * rows + iota((rows, n_o), 0)
        occ_j = pick(iota((rows, n_o), 1) == lax.div(line, W), occ_row, 1)
        ewin_b = pick(iota((rows, W), 1) == lax.rem(iota((rows, W), 0), W), ewin_row, 1)
        cden[...] = occ_j - ewin_b
        for i in range(cols // n_v):
            at = g * (cols // n_v) + i
            rden[:, i * n_v:(i + 1) * n_v] = pick(iota((1, n_o), 1) == at, occ_row, 1) - vir_row
        pair = plist[...]
        o_i = pick(iota((n_o, n_pairs), 0) == lax.div(pair, n_o), occ_col, 0)
        o_j = pick(iota((n_o, n_pairs), 0) == lax.rem(pair, n_o), occ_col, 0)
        ab = iota((W * W, W), 0)
        e_a = pick(iota((W * W, W), 1) == lax.div(ab, W), ewin_row, 1)
        e_b = pick(iota((W * W, W), 1) == lax.rem(ab, W), ewin_row, 1)
        lden[...] = (o_i + o_j) - (e_a + e_b)

    def spread(buf, slot, send, recv, k):
        q = q_of[k]
        return pltpu.make_async_remote_copy(
            src_ref=buf.at[slot], dst_ref=buf.at[slot], send_sem=send.at[k], recv_sem=recv.at[slot],
            device_id={"pair": q}, device_id_type=MESH,
        )

    def spread_all(buf, send, recv):
        for k in range(n_p - 1):
            spread(buf, p, send, recv, k).start()

    def spread_wait(buf, send, recv):
        for k in range(n_p - 1):
            spread(buf, q_of[k], send, recv, k).wait_recv()

    def tile_part():
        total = None
        for q in range(n_p):
            term = dot_nt(xbuf[q], ybuf[q].reshape(n_g * own_c, ybuf.shape[3]))
            total = term if total is None else total + term
        zbuf[p] = total.astype(zbuf.dtype)

    def weights():
        for j in range(own_c // SUB):
            for a in range(W):
                for b in range(W):
                    at = (a * W + b) * SUB
                    wt[j, at:at + SUB, :] = zbuf[b, a * own_c + j * SUB:a * own_c + (j + 1) * SUB, :]

    piece = n_pairs // n_z

    def ladder_piece(i):
        at = pl.ds(pl.multiple_of(i * piece, 8), piece)
        total = None
        for j in range(own_c // SUB):
            lhs = tbuf[at, j * SUB:(j + 1) * SUB, :].reshape(piece * SUB, tbuf.shape[2])
            term = dot_nt(lhs, wt[j])
            total = term if total is None else total + term
        total = total.reshape(piece, SUB, W * W * SUB)
        r_id = lax.broadcasted_iota(jnp.int32, (1, SUB, W * W * SUB), 1)
        c_id = lax.broadcasted_iota(jnp.int32, (1, SUB, W * W * SUB), 2)
        sbuf[at, :] = jnp.sum(jnp.where(r_id == c_id % SUB, total, 0.0), axis=1)

    def lad_copy(k, slot):
        return pltpu.make_async_remote_copy(
            src_ref=lbuf.at[slot], dst_ref=lbuf.at[slot], send_sem=lsend.at[k], recv_sem=lrecv.at[slot],
            device_id={"grid": g_of[k]}, device_id_type=MESH,
        )

    def ladder_send():
        row = lax.broadcasted_iota(jnp.int32, (W * W, W * W * SUB), 0)
        col = lax.broadcasted_iota(jnp.int32, (W * W, W * W * SUB), 1)
        ones = jnp.where(row == col // SUB, 1.0, 0.0).astype(jnp.float32)
        lbuf[g] = lax.dot_general(
            ones, sbuf[...], NT, precision=lax.Precision.HIGHEST, preferred_element_type=jnp.float32
        )
        for k in range(n_g - 1):
            lad_copy(k, g).start()

    def ladder_end():
        for k in range(n_g - 1):
            lad_copy(k, g_of[k]).wait_recv()
        total = lbuf[0]
        for s in range(1, n_g):
            total = total + lbuf[s]
        lad_out[...] = total / lden[...]

    def chunk(r, before, extra):
        product(r, g, first=True)
        if r == 0:
            spread_wait(xbuf, xsend, xrecv)
            mine = pl.ds(pl.multiple_of(p * own_c, SUB), own_c)
            ybuf[:, g] = xbuf[:, mine, :]
            own_send(item_y, begin)
        hop(r, sib, 1, sib).wait_recv()
        product(r, sib)
        before()

        def step(t, carry):
            forward(r, t, True, begin)
            if r == 0:
                forward(item_y, t, True, begin)
            if r + 1 < CHUNKS:
                @pl.when(t == 1)
                def _():
                    own_send(r + 1, begin)
            extra(t)

            def use(d, sz):
                product(r, sz * 2 + c)
                s = sz * 2 + 1 - c
                hop(r, s, 1, sib).wait_recv()
                product(r, s)

            each_line(t, use)
            return carry

        lax.fori_loop(1, n_z, step, 0)
        reduce_start(r)

    load_x.wait()
    spread_all(xbuf, xsend, xrecv)
    load_a.wait()
    own_send(0, begin)
    chunk(0, denominators, lambda t: None)
    hop(item_y, sib, 1, sib).wait_recv()

    def rest(t, carry):
        each_line(t, lambda d, sz: hop(item_y, sz * 2 + 1 - c, 1, sib).wait_recv())
        return carry

    lax.fori_loop(1, n_z, rest, 0)
    tile_part()
    spread_all(zbuf, zsend, zrecv)

    def ladder_begin():
        spread_wait(zbuf, zsend, zrecv)
        weights()
        load_t.wait()
        ladder_piece(0)
        ladder_piece(n_z - 1)

    def ladder_next(t):
        @pl.when(t < n_z - 1)
        def _():
            ladder_piece(t)

        @pl.when(t == n_z - 1)
        def _():
            ladder_send()

    for r in range(1, CHUNKS):
        chunk(
            r,
            ladder_begin if r == 1 else (lambda: None),
            ladder_next if r == 1 else (lambda t: None),
        )
        reduce_end(r - 1)
    ladder_end()
    reduce_end(CHUNKS - 1)

    def sent(cp):
        cp.wait_send()

    for item in range(CHUNKS + 1):
        own_send(item, sent)

        def step(t, carry, item=item):
            forward(item, t, False, sent)
            return carry

        lax.fori_loop(1, n_z, step, 0)
    for k in range(n_p - 1):
        spread(xbuf, p, xsend, xrecv, k).wait_send()
        spread(zbuf, p, zsend, zrecv, k).wait_send()
        for r in range(CHUNKS):
            for i in range(tiles):
                scatter(r, i, k, q_of[k], p).wait_send()
    for k in range(n_g - 1):
        lad_copy(k, g).wait_send()


def tile_of(cols):
    return 1024 if cols % 1024 == 0 else cols


def fused(n_p, n_g, amplitudes, cycle_matrix, fit_panel, pair_amps, *small):
    rows = amplitudes.shape[0] // n_p
    depth = amplitudes.shape[1]
    cols = cycle_matrix.shape[0]
    n_pairs, own_c, n_v = pair_amps.shape
    aux = fit_panel.shape[2]
    h = rows // CHUNKS
    tiles = cols // tile_of(cols)
    bf, f32 = jnp.bfloat16, jnp.float32
    dma = pltpu.SemaphoreType.DMA
    hbm = pl.BlockSpec(memory_space=pl.ANY)
    vmem = pl.BlockSpec(memory_space=pltpu.VMEM)
    return pl.pallas_call(
        functools.partial(kernel, n_p, n_g),
        out_shape=(
            jax.ShapeDtypeStruct((rows, cols), bf),
            jax.ShapeDtypeStruct((W * W, n_pairs), f32),
        ),
        in_specs=[hbm] * 4 + [vmem] * 4,
        out_specs=(vmem, vmem),
        scratch_shapes=[
            pltpu.VMEM((n_g, n_p, rows, depth), bf),
            pltpu.VMEM((n_g, cols, depth), bf),
            pltpu.VMEM((n_pairs, own_c, n_v), bf),
            pltpu.VMEM((n_p, W * own_c, aux), bf),
            pltpu.VMEM((n_p, n_g, own_c, aux), bf),
            pltpu.VMEM((n_p, W * own_c, n_v), bf),
            pltpu.VMEM((own_c // SUB, W * W * SUB, n_v), bf),
            pltpu.VMEM((n_pairs, W * W * SUB), f32),
            pltpu.VMEM((n_g, W * W, n_pairs), f32),
            pltpu.VMEM((cols, n_p * h), f32),
            pltpu.VMEM((CHUNKS, n_p, h, cols), f32),
            pltpu.VMEM((CHUNKS, n_p, h, cols), bf),
            pltpu.VMEM((n_p, CHUNKS, h, cols), bf),
            pltpu.VMEM((rows, 1), f32),
            pltpu.VMEM((1, cols), f32),
            pltpu.VMEM((W * W, n_pairs), f32),
            dma((n_g,)),
            dma((3,)),
            dma((CHUNKS + 1, n_g)),
            dma((CHUNKS + 1, n_g, 3)),
            dma((n_p,)),
            dma((n_p,)),
            dma((n_p,)),
            dma((n_p,)),
            dma((CHUNKS, tiles, n_p)),
            dma((CHUNKS, tiles, n_p)),
            dma((n_g,)),
            dma((n_g,)),
        ],
        compiler_params=pltpu.CompilerParams(
            collective_id=0, has_side_effects=True, vmem_limit_bytes=63 * 1024 * 1024
        ),
    )(
        amplitudes.reshape(n_p, rows, depth),
        cycle_matrix,
        fit_panel.reshape(W * own_c, aux),
        pair_amps,
        *[x.reshape(1, x.shape[0]) for x in small],
    )


def plain(amplitudes, cycle_matrix, fit_panel, pair_amps):
    partial_cycle = lax.dot_general(
        lax.all_gather(amplitudes, "grid", axis=1, tiled=True),
        cycle_matrix,
        NT,
        preferred_element_type=jnp.float32,
    )
    cycle_sum = lax.psum_scatter(partial_cycle, "pair", scatter_dimension=0, tiled=True)
    full_aux = lax.all_gather(fit_panel, "pair", axis=2, tiled=True)
    tile = jnp.einsum(
        "acq,bdq->abcd",
        full_aux,
        lax.all_gather(full_aux, "grid", axis=1, tiled=True),
        preferred_element_type=jnp.float32,
    ).astype(jnp.bfloat16)
    flat_amps = pair_amps.reshape(pair_amps.shape[0], pair_amps.shape[1] * pair_amps.shape[2])
    flat_tile = tile.reshape(W * W, tile.shape[2] * tile.shape[3])
    partial_ladder = lax.dot_general(
        flat_amps, flat_tile, NT, preferred_element_type=jnp.float32
    )
    return cycle_sum, lax.psum(partial_ladder, "grid")


def suits(n_p, n_g, amplitudes, cycle_matrix, fit_panel, pair_amps):
    rows = amplitudes.shape[0] // n_p
    return (
        n_p == W
        and n_g % 2 == 0
        and rows % (CHUNKS * SUB) == 0
        and n_p * rows % (CHUNKS * 128) == 0
        and cycle_matrix.shape[0] % pair_amps.shape[2] == 0
        and amplitudes.shape[1] % 128 == 0
        and fit_panel.shape[2] % 128 == 0
        and pair_amps.shape[1] % SUB == 0
        and pair_amps.shape[2] % 128 == 0
        and pair_amps.shape[0] % (8 * (n_g // 2)) == 0
    )


def local(
    n_p, n_g,
    cycle_matrix, amplitudes, fit_panel, pair_amps, pair_list, window_list, occ_energy, vir_energy
):
    arrays = (amplitudes, cycle_matrix, fit_panel, pair_amps)
    if suits(n_p, n_g, *arrays):
        cycle_update, ladder = fused(
            n_p, n_g, *arrays, pair_list, window_list, occ_energy, vir_energy
        )
        return cycle_update, ladder.T
    window_energy = lookup(vir_energy, window_list[:W])
    local_rows = cycle_matrix.shape[0]
    cycle_sum, ladder = plain(*arrays)
    column_ids = lax.axis_index("pair") * cycle_sum.shape[0] + jnp.arange(
        cycle_sum.shape[0], dtype=jnp.int32
    )
    row_ids = lax.axis_index("grid") * local_rows + jnp.arange(local_rows, dtype=jnp.int32)
    col_energy = lookup(occ_energy, column_ids // W) - lookup(window_energy, column_ids % W)
    row_energy = lookup(occ_energy, row_ids // V) - lookup(vir_energy, row_ids % V)
    cycle_update = (cycle_sum / (col_energy[:, None] + row_energy[None, :])).astype(jnp.bfloat16)
    pair_energy = lookup(occ_energy, pair_list // O) + lookup(occ_energy, pair_list % O)
    win_pair = (window_energy[:, None] + window_energy[None, :]).reshape(W * W)
    ladder_update = ladder / (pair_energy[:, None] - win_pair[None, :])
    return (cycle_update, ladder_update)


def solution(mesh):
    return jax.shard_map(
        functools.partial(local, mesh.shape["pair"], mesh.shape["grid"]),
        mesh=mesh,
        in_specs=(
            P("grid", "pair"),
            P(None, ("pair", "grid")),
            P(None, "grid", "pair"),
            P("pair", "grid", None),
            P("pair"),
            P(),
            P(),
            P(),
        ),
        out_specs=(P("pair", "grid"), P("pair", None)),
        check_vma=False,
    )
```

```python
import functools

import jax
import jax.numpy as jnp
from jax import lax
from jax.experimental import pallas as pl
from jax.experimental.pallas import tpu as pltpu
from jax.sharding import PartitionSpec as P

O = 64
V = 384
W = 4
CHUNKS = 2
SUB = 16
MESH = pl.DeviceIdType.MESH
NT = (((1,), (1,)), ((), ()))


def lookup(table, index):
    hits = index[:, None] == jnp.arange(table.shape[0], dtype=jnp.int32)[None, :]
    return jnp.sum(jnp.where(hits, table[None, :], jnp.float32(0.0)), axis=1)


def dot_nt(a, b):
    return lax.dot_general(a, b, NT, preferred_element_type=jnp.float32)


def kernel(
    n_p, n_g, amps, mat, fit, pairs, plist, wlist, occ, vir, cyc_out, lad_out,
    abuf, mbuf, tbuf, xbuf, ybuf, zbuf, wt, sbuf, lbuf, acc, part, rsend, rrecv, cden, rden, lden,
    msem, lsem, arecv, asend, xrecv, xsend, zrecv, zsend, rrsem, rssem, lrecv, lsend,
):
    n_z = n_g // 2
    p = lax.axis_index("pair")
    g = lax.axis_index("grid")
    z = g // 2
    c = g % 2
    sib = z * 2 + 1 - c
    rows = abuf.shape[2]
    depth = abuf.shape[3]
    h = rows // CHUNKS
    cols = mbuf.shape[1]
    own_c = ybuf.shape[2]
    n_pairs = tbuf.shape[0]
    item_y = CHUNKS
    tile_n = tile_of(cols)
    tiles = cols // tile_n
    q_of = [lax.rem(p + k, n_p) for k in range(1, n_p)]
    g_of = [lax.rem(g + k, n_g) for k in range(1, n_g)]

    load_x = pltpu.make_async_copy(fit, xbuf.at[p], lsem.at[0])
    load_x.start()
    load_a = pltpu.make_async_copy(amps, abuf.at[g], lsem.at[1])
    load_a.start()

    def load_m(s):
        at = pl.multiple_of(s * depth, 128)
        return pltpu.make_async_copy(mat.at[:, pl.ds(at, depth)], mbuf.at[s], msem.at[s])

    load_m(g).start()
    load_m(sib).start()
    load_t = pltpu.make_async_copy(pairs, tbuf, lsem.at[2])

    def load_far(ts):
        for t in ts:
            for d in (1, -1):
                sz = z - d * t

                @pl.when(jnp.logical_and(sz >= 0, sz < n_z))
                def _(sz=sz):
                    load_m(sz * 2 + c).start()
                    load_m(sz * 2 + 1 - c).start()

    barrier = pltpu.get_barrier_semaphore()
    for q in q_of:
        pl.semaphore_signal(barrier, inc=1, device_id={"pair": q}, device_id_type=MESH)
    for q in g_of:
        pl.semaphore_signal(barrier, inc=1, device_id={"grid": q}, device_id_type=MESH)
    pl.semaphore_wait(barrier, n_p - 1 + n_g - 1)

    def shard(item, s):
        if item == item_y:
            return ybuf.at[:, s]
        return abuf.at[s, :, pl.ds(item * h, h), :]

    def hop(item, s, kind, target):
        ref = shard(item, s)
        return pltpu.make_async_remote_copy(
            src_ref=ref, dst_ref=ref, send_sem=asend.at[item, s, kind], recv_sem=arecv.at[item, s],
            device_id={"grid": target}, device_id_type=MESH,
        )

    reach = max(1, n_z // 2)
    near, far = range(1, reach + 1), range(reach + 1, n_z)

    def own_send(item, act):
        act(hop(item, g, 0, sib))
        for t in near:
            for j, d in enumerate((1, -1)):
                to = z + d * t

                @pl.when(jnp.logical_and(to >= 0, to < n_z))
                def _(t=t, j=j, to=to):
                    act(hop(item, g, 2 + j * reach + t - 1, to * 2 + c))

    def each_line(t, body):
        for d in (1, -1):
            sz = z - d * t

            @pl.when(jnp.logical_and(sz >= 0, sz < n_z))
            def _(d=d, sz=sz):
                body(d, sz)

    def forward(item, t, wait_first, act):
        def body(d, sz):
            s = sz * 2 + c
            if wait_first:
                hop(item, s, 0, sib).wait_recv()
            if t >= reach:
                nz = z + d

                @pl.when(jnp.logical_and(nz >= 0, nz < n_z))
                def _():
                    act(hop(item, s, 1, nz * 2 + c))

            act(hop(item, s, 0, sib))

        each_line(t, body)

    def begin(cp):
        cp.start()

    def product_tile(r, s, i, first=False):
        at = pl.ds(i * tile_n if isinstance(i, int) else pl.multiple_of(i * tile_n, 128), tile_n)
        rhs = abuf[s, :, r * h:(r + 1) * h, :].reshape(n_p * h, depth)
        out = dot_nt(mbuf[s, at, :], rhs)
        if first:
            acc[at, :] = out
        else:
            acc[at, :] += out

    def product(r, s, first=False):
        if r == 0:
            load_m(s).wait()

        def tile(i, carry):
            product_tile(r, s, i, first)
            return carry

        lax.fori_loop(0, tiles, tile, 0)

    def scatter(r, i, k, q, slot):
        at = slice(i * tile_n, (i + 1) * tile_n)
        return pltpu.make_async_remote_copy(
            src_ref=rsend.at[r, q, :, at], dst_ref=rrecv.at[slot, r, :, at],
            send_sem=rssem.at[r, i, k], recv_sem=rrsem.at[r, i, slot],
            device_id={"pair": q}, device_id_type=MESH,
        )

    def reduce_start(r, last):
        for i in range(tiles):
            last(i)
            at = slice(i * tile_n, (i + 1) * tile_n)
            block = acc[at, :].T.reshape(n_p, h, tile_n)
            part[r, :, :, at] = block
            rsend[r, :, :, at] = block.astype(rsend.dtype)
            for k in range(n_p - 1):
                scatter(r, i, k, q_of[k], p).start()

    def reduce_end(r):
        for i in range(tiles):
            at = slice(i * tile_n, (i + 1) * tile_n)
            total = part[r, p, :, at]
            for q in q_of:
                scatter(r, i, 0, q, q).wait_recv()
                total = total + rrecv[q, r, :, at].astype(jnp.float32)
            low = cden[r * h:(r + 1) * h, :] + rden[:, at]
            cyc_out[r * h:(r + 1) * h, at] = (total / low).astype(cyc_out.dtype)

    def iota(shape, dim):
        return lax.broadcasted_iota(jnp.int32, shape, dim)

    def pick(hits, values, axis):
        return jnp.sum(jnp.where(hits, values, jnp.zeros_like(values)), axis=axis, keepdims=True)

    def denominators():
        n_o, n_v = occ.shape[1], vir.shape[1]
        occ_row, vir_row = occ[...], vir[...]
        want = pick(iota((W, n_v), 0) == iota((W, n_v), 1), wlist[...], 1)
        ewin_col = pick(iota((W, n_v), 1) == want, vir_row, 1)
        ewin_row = pick(iota((W, W), 0) == iota((W, W), 1), ewin_col, 0)
        occ_col = pick(iota((n_o, n_o), 0) == iota((n_o, n_o), 1), occ_row, 1)
        line = p * rows + iota((rows, n_o), 0)
        occ_j = pick(iota((rows, n_o), 1) == lax.div(line, W), occ_row, 1)
        ewin_b = pick(iota((rows, W), 1) == lax.rem(iota((rows, W), 0), W), ewin_row, 1)
        cden[...] = occ_j - ewin_b
        for i in range(cols // n_v):
            at = g * (cols // n_v) + i
            rden[:, i * n_v:(i + 1) * n_v] = pick(iota((1, n_o), 1) == at, occ_row, 1) - vir_row
        pair = plist[...]
        o_i = pick(iota((n_o, n_pairs), 0) == lax.div(pair, n_o), occ_col, 0)
        o_j = pick(iota((n_o, n_pairs), 0) == lax.rem(pair, n_o), occ_col, 0)
        ab = iota((W * W, W), 0)
        e_a = pick(iota((W * W, W), 1) == lax.div(ab, W), ewin_row, 1)
        e_b = pick(iota((W * W, W), 1) == lax.rem(ab, W), ewin_row, 1)
        lden[...] = (o_i + o_j) - (e_a + e_b)

    def spread(buf, slot, send, recv, k):
        q = q_of[k]
        return pltpu.make_async_remote_copy(
            src_ref=buf.at[slot], dst_ref=buf.at[slot], send_sem=send.at[k], recv_sem=recv.at[slot],
            device_id={"pair": q}, device_id_type=MESH,
        )

    def spread_all(buf, send, recv):
        for k in range(n_p - 1):
            spread(buf, p, send, recv, k).start()

    def spread_wait(buf, send, recv):
        for k in range(n_p - 1):
            spread(buf, q_of[k], send, recv, k).wait_recv()

    def tile_part():
        total = None
        for q in range(n_p):
            term = dot_nt(xbuf[q], ybuf[q].reshape(n_g * own_c, ybuf.shape[3]))
            total = term if total is None else total + term
        zbuf[p] = total.astype(zbuf.dtype)

    def weights():
        for j in range(own_c // SUB):
            for a in range(W):
                for b in range(W):
                    at = (a * W + b) * SUB
                    wt[j, at:at + SUB, :] = zbuf[b, a * own_c + j * SUB:a * own_c + (j + 1) * SUB, :]

    piece = n_pairs // n_z

    def ladder_piece(i):
        at = pl.ds(pl.multiple_of(i * piece, 8), piece)
        total = None
        for j in range(own_c // SUB):
            lhs = tbuf[at, j * SUB:(j + 1) * SUB, :].reshape(piece * SUB, tbuf.shape[2])
            term = dot_nt(lhs, wt[j])
            total = term if total is None else total + term
        total = total.reshape(piece, SUB, W * W * SUB)
        r_id = lax.broadcasted_iota(jnp.int32, (1, SUB, W * W * SUB), 1)
        c_id = lax.broadcasted_iota(jnp.int32, (1, SUB, W * W * SUB), 2)
        sbuf[at, :] = jnp.sum(jnp.where(r_id == c_id % SUB, total, 0.0), axis=1)

    def lad_copy(k, slot):
        return pltpu.make_async_remote_copy(
            src_ref=lbuf.at[slot], dst_ref=lbuf.at[slot], send_sem=lsend.at[k], recv_sem=lrecv.at[slot],
            device_id={"grid": g_of[k]}, device_id_type=MESH,
        )

    def ladder_send():
        row = lax.broadcasted_iota(jnp.int32, (W * W, W * W * SUB), 0)
        col = lax.broadcasted_iota(jnp.int32, (W * W, W * W * SUB), 1)
        ones = jnp.where(row == col // SUB, 1.0, 0.0).astype(jnp.float32)
        lbuf[g] = lax.dot_general(
            ones, sbuf[...], NT, precision=lax.Precision.HIGHEST, preferred_element_type=jnp.float32
        )
        for k in range(n_g - 1):
            lad_copy(k, g).start()

    def ladder_end():
        for k in range(n_g - 1):
            lad_copy(k, g_of[k]).wait_recv()
        total = lbuf[0]
        for s in range(1, n_g):
            total = total + lbuf[s]
        lad_out[...] = total / lden[...]

    def use(r, t):
        def body(d, sz):
            product(r, sz * 2 + c)
            s = sz * 2 + 1 - c
            hop(r, s, 0, sib).wait_recv()
            product(r, s)

        each_line(t, body)

    def use_last(r):
        if len(far) == 0:
            return lambda i: None
        t = far[-1]

        def arrive(d, sz):
            s = sz * 2 + 1 - c
            hop(r, s, 0, sib).wait_recv()
            if r == 0:
                load_m(s).wait()
                load_m(sz * 2 + c).wait()

        each_line(t, arrive)

        def last(i):
            def body(d, sz):
                product_tile(r, sz * 2 + c, i)
                product_tile(r, sz * 2 + 1 - c, i)

            each_line(t, body)

        return last

    load_x.wait()
    spread_all(xbuf, xsend, xrecv)
    load_a.wait()
    own_send(0, begin)
    load_far(near[:1])
    denominators()
    spread_wait(xbuf, xsend, xrecv)
    mine = pl.ds(pl.multiple_of(p * own_c, SUB), own_c)
    ybuf[:, g] = xbuf[:, mine, :]
    own_send(item_y, begin)

    for r in range(CHUNKS):
        product(r, g, first=True)
        if r == 0:
            load_far(range(2, n_z))
        for t in near:
            forward(r, t, True, begin)
        if r == 0:
            for t in near:
                forward(item_y, t, True, begin)
            load_t.start()
        if r + 1 < CHUNKS:
            own_send(r + 1, begin)
        hop(r, sib, 0, sib).wait_recv()
        product(r, sib)
        for t in near:
            use(r, t)
        if r == 0:
            for t in far:
                forward(item_y, t, True, begin)
            hop(item_y, sib, 0, sib).wait_recv()
            for t in range(1, n_z):
                each_line(t, lambda d, sz: hop(item_y, sz * 2 + 1 - c, 0, sib).wait_recv())
            tile_part()
            spread_all(zbuf, zsend, zrecv)
        if r == 1:
            spread_wait(zbuf, zsend, zrecv)
            weights()
            load_t.wait()

            def pieces(i, carry):
                ladder_piece(i)
                return carry

            lax.fori_loop(0, n_z, pieces, 0)
            ladder_send()
        for t in far:
            forward(r, t, True, begin)
            if t != far[-1]:
                use(r, t)
        reduce_start(r, use_last(r))
        if r >= 1:
            reduce_end(r - 1)
    ladder_end()
    reduce_end(CHUNKS - 1)

    def sent(cp):
        cp.wait_send()

    for item in range(CHUNKS + 1):
        own_send(item, sent)
        for t in range(1, n_z):
            forward(item, t, False, sent)
    for k in range(n_p - 1):
        spread(xbuf, p, xsend, xrecv, k).wait_send()
        spread(zbuf, p, zsend, zrecv, k).wait_send()
        for r in range(CHUNKS):
            for i in range(tiles):
                scatter(r, i, k, q_of[k], p).wait_send()
    for k in range(n_g - 1):
        lad_copy(k, g).wait_send()


def tile_of(cols):
    return 1024 if cols % 1024 == 0 else cols


def fused(n_p, n_g, amplitudes, cycle_matrix, fit_panel, pair_amps, *small):
    rows = amplitudes.shape[0] // n_p
    depth = amplitudes.shape[1]
    cols = cycle_matrix.shape[0]
    n_pairs, own_c, n_v = pair_amps.shape
    aux = fit_panel.shape[2]
    h = rows // CHUNKS
    tiles = cols // tile_of(cols)
    bf, f32 = jnp.bfloat16, jnp.float32
    dma = pltpu.SemaphoreType.DMA
    hbm = pl.BlockSpec(memory_space=pl.ANY)
    vmem = pl.BlockSpec(memory_space=pltpu.VMEM)
    return pl.pallas_call(
        functools.partial(kernel, n_p, n_g),
        out_shape=(
            jax.ShapeDtypeStruct((rows, cols), bf),
            jax.ShapeDtypeStruct((W * W, n_pairs), f32),
        ),
        in_specs=[hbm] * 4 + [vmem] * 4,
        out_specs=(vmem, vmem),
        scratch_shapes=[
            pltpu.VMEM((n_g, n_p, rows, depth), bf),
            pltpu.VMEM((n_g, cols, depth), bf),
            pltpu.VMEM((n_pairs, own_c, n_v), bf),
            pltpu.VMEM((n_p, W * own_c, aux), bf),
            pltpu.VMEM((n_p, n_g, own_c, aux), bf),
            pltpu.VMEM((n_p, W * own_c, n_v), bf),
            pltpu.VMEM((own_c // SUB, W * W * SUB, n_v), bf),
            pltpu.VMEM((n_pairs, W * W * SUB), f32),
            pltpu.VMEM((n_g, W * W, n_pairs), f32),
            pltpu.VMEM((cols, n_p * h), f32),
            pltpu.VMEM((CHUNKS, n_p, h, cols), f32),
            pltpu.VMEM((CHUNKS, n_p, h, cols), bf),
            pltpu.VMEM((n_p, CHUNKS, h, cols), bf),
            pltpu.VMEM((rows, 1), f32),
            pltpu.VMEM((1, cols), f32),
            pltpu.VMEM((W * W, n_pairs), f32),
            dma((n_g,)),
            dma((3,)),
            dma((CHUNKS + 1, n_g)),
            dma((CHUNKS + 1, n_g, 2 + 2 * max(1, n_g // 4))),
            dma((n_p,)),
            dma((n_p,)),
            dma((n_p,)),
            dma((n_p,)),
            dma((CHUNKS, tiles, n_p)),
            dma((CHUNKS, tiles, n_p)),
            dma((n_g,)),
            dma((n_g,)),
        ],
        compiler_params=pltpu.CompilerParams(
            collective_id=0, has_side_effects=True, vmem_limit_bytes=63 * 1024 * 1024
        ),
    )(
        amplitudes.reshape(n_p, rows, depth),
        cycle_matrix,
        fit_panel.reshape(W * own_c, aux),
        pair_amps,
        *[x.reshape(1, x.shape[0]) for x in small],
    )


def plain(amplitudes, cycle_matrix, fit_panel, pair_amps):
    partial_cycle = lax.dot_general(
        lax.all_gather(amplitudes, "grid", axis=1, tiled=True),
        cycle_matrix,
        NT,
        preferred_element_type=jnp.float32,
    )
    cycle_sum = lax.psum_scatter(partial_cycle, "pair", scatter_dimension=0, tiled=True)
    full_aux = lax.all_gather(fit_panel, "pair", axis=2, tiled=True)
    tile = jnp.einsum(
        "acq,bdq->abcd",
        full_aux,
        lax.all_gather(full_aux, "grid", axis=1, tiled=True),
        preferred_element_type=jnp.float32,
    ).astype(jnp.bfloat16)
    flat_amps = pair_amps.reshape(pair_amps.shape[0], pair_amps.shape[1] * pair_amps.shape[2])
    flat_tile = tile.reshape(W * W, tile.shape[2] * tile.shape[3])
    partial_ladder = lax.dot_general(
        flat_amps, flat_tile, NT, preferred_element_type=jnp.float32
    )
    return cycle_sum, lax.psum(partial_ladder, "grid")


def suits(n_p, n_g, amplitudes, cycle_matrix, fit_panel, pair_amps):
    rows = amplitudes.shape[0] // n_p
    return (
        n_p == W
        and n_g % 2 == 0
        and rows % (CHUNKS * SUB) == 0
        and n_p * rows % (CHUNKS * 128) == 0
        and cycle_matrix.shape[0] % pair_amps.shape[2] == 0
        and amplitudes.shape[1] % 128 == 0
        and fit_panel.shape[2] % 128 == 0
        and pair_amps.shape[1] % SUB == 0
        and pair_amps.shape[2] % 128 == 0
        and pair_amps.shape[0] % (8 * (n_g // 2)) == 0
    )


def local(
    n_p, n_g,
    cycle_matrix, amplitudes, fit_panel, pair_amps, pair_list, window_list, occ_energy, vir_energy
):
    arrays = (amplitudes, cycle_matrix, fit_panel, pair_amps)
    if suits(n_p, n_g, *arrays):
        cycle_update, ladder = fused(
            n_p, n_g, *arrays, pair_list, window_list, occ_energy, vir_energy
        )
        return cycle_update, ladder.T
    window_energy = lookup(vir_energy, window_list[:W])
    local_rows = cycle_matrix.shape[0]
    cycle_sum, ladder = plain(*arrays)
    column_ids = lax.axis_index("pair") * cycle_sum.shape[0] + jnp.arange(
        cycle_sum.shape[0], dtype=jnp.int32
    )
    row_ids = lax.axis_index("grid") * local_rows + jnp.arange(local_rows, dtype=jnp.int32)
    col_energy = lookup(occ_energy, column_ids // W) - lookup(window_energy, column_ids % W)
    row_energy = lookup(occ_energy, row_ids // V) - lookup(vir_energy, row_ids % V)
    cycle_update = (cycle_sum / (col_energy[:, None] + row_energy[None, :])).astype(jnp.bfloat16)
    pair_energy = lookup(occ_energy, pair_list // O) + lookup(occ_energy, pair_list % O)
    win_pair = (window_energy[:, None] + window_energy[None, :]).reshape(W * W)
    ladder_update = ladder / (pair_energy[:, None] - win_pair[None, :])
    return (cycle_update, ladder_update)


def solution(mesh):
    return jax.shard_map(
        functools.partial(local, mesh.shape["pair"], mesh.shape["grid"]),
        mesh=mesh,
        in_specs=(
            P("grid", "pair"),
            P(None, ("pair", "grid")),
            P(None, "grid", "pair"),
            P("pair", "grid", None),
            P("pair"),
            P(),
            P(),
            P(),
        ),
        out_specs=(P("pair", "grid"), P("pair", None)),
        check_vma=False,
    )
```
